32 devices in a mesh: job: 2 (over y), tile: 4 (over z), src: 4 (over x, core).
Axes of the slice: x: 2, y: 2, z: 4, core: 2. Of those that a mesh axis runs over, the one named last changes fastest.
Arguments:
- forward_field: float32 [8, 2, 16, 256, 128], P(('job', 'src'), None, 'tile'), parts along dimension 0, may hold values from -6 to 6
- adjoint_guess: float32 [8, 2, 16, 256, 128], P(('job', 'src'), None, 'tile'), parts along dimension 0, may hold values from -6 to 6
- conductivity: float32 [32, 256, 128], P(('job', 'tile')), parts along dimension 0, may hold values from 0.3 to 3
- freq_kappa: float32 [8], P('job'), parts along dimension 0, may hold values from 0.5 to 4
- pair_freq: int32 [8], P(('job', 'src')), parts along dimension 0, may hold values from 0 to 3
- recv_data: float32 [8, 2, 256], P(('job', 'src')), parts along dimension 0, may hold values from -6 to 6
- recv_weights: float32 [512, 64], P('job'), parts along dimension 0, may hold values from 0.05 to 1
- recv_x: int32 [512], P('job'), parts along dimension 0, may hold values from 0 to 12
- recv_y: int32 [512], P('job'), parts along dimension 0, may hold values from 0 to 252
- recv_z: int32 [512], P('job'), parts along dimension 0, may hold values from 0 to 124
Outputs:
- adjoint: float32 [8, 2, 16, 256, 128], P(('job', 'src'), None, 'tile'), parts along dimension 0
- gradient: float32 [32, 256, 128], P(('job', 'tile'), 'src'), parts along dimension 0
The draws below stay inside these ranges and needn't reach their ends.
There are 2 independent parts, one for each index of `job`. The reference program is written for one: setup_inputs(seed, part) draws one part's arguments, and reference() takes and returns one part's arrays. A program takes and returns all parts, laid end to end along the dimension named above; each array names one. Nothing has to cross between parts.
Inputs may be any that keep to these rules, and one draw needn't show every extreme that they name: `recv_x`: each receiver's block of 4 x 4 x 4 cells lies inside the grid along the first dimension. `recv_y`: each receiver's block lies inside the grid along the second dimension. `recv_z`: each receiver's block lies inside the grid along the third dimension. `pair_freq`: an index into freq_kappa.
All inputs are finite; a program needn't handle non-finite values.
Results may differ from the reference program's by a relative error of at most 0.00011.
Values sent between devices are 32-bit elements; how exact they have to be, the bound alone decides.
A program may use at most 64 MiB of HBM per device.

```python
import math
import jax
import jax.numpy as jnp
from jax import lax

NY = 256
NZ = 128
RECV = 256
NF = 4
NX = 16
PAIRS = 4


def place_ends(values, stream_key, smallest, high):
    extent = values.shape
    spot = [jax.random.randint(jax.random.fold_in(stream_key, axis), (), 0, extent[axis]) for axis in range(len(extent))]
    values = values.at[tuple(spot)].set(smallest)
    longest = extent.index(max(extent))
    spot[longest] = (spot[longest] + 1) % extent[longest]
    return values.at[tuple(spot)].set(high)


def shard_levels(rng, shape, cuts, smallest, largest):
    def one(position, shards_of):
        draws = jax.random.uniform(jax.random.fold_in(jax.random.fold_in(rng, 6), position), (shards_of,), jnp.float32, smallest / len(cuts), largest / len(cuts))
        return jnp.repeat(jnp.exp(draws), shape[position] // shards_of).reshape((-1,) + (1,) * (len(shape) - position - 1))

    factor_of = one(*cuts[0])
    for cut in cuts[1:]:
        factor_of = factor_of * one(*cut)
    return factor_of


def gaussian(stream_key, extent, spread, reach, pieces=(), kind=jnp.bfloat16):
    level = shard_levels(stream_key, extent, pieces, -0.22, 0.18) if pieces else 1.0
    drawn = jax.random.normal(stream_key, extent, jnp.float32) * spread * level
    return jnp.minimum(jnp.maximum(drawn, -reach), reach).astype(kind)


def setup_inputs(seed: int = 0, part: int = 0) -> dict:
    key_of = jax.random.split(jax.random.key(seed), 11)
    part_splits = jax.random.split(jax.random.fold_in(key_of[10], part), 11)
    forward_field = gaussian(part_splits[0], (PAIRS, 2, NX, NY, NZ), 1.0, 6.0, ((0, 4), (2, 4)), jnp.float32)
    adjoint_guess = gaussian(part_splits[1], (PAIRS, 2, NX, NY, NZ), 1.0, 6.0, ((0, 4), (2, 4)), jnp.float32)
    conductivity = jnp.clip(jnp.exp(math.log(3.0) - 2.3025851 * jax.random.uniform(part_splits[2], (NX, NY, NZ), jnp.float32) ** shard_levels(part_splits[2], (NX, NY, NZ), ((0, 4),), -0.2, 0.2)), 0.3, 3.0)
    freq_kappa = jnp.clip(jnp.exp(jax.random.uniform(part_splits[3], (NF,), jnp.float32, math.log(0.5), math.log(4.0))), 0.5, 4.0)
    pair_freq = place_ends(jax.random.randint(part_splits[4], (PAIRS,), 0, NF), jax.random.fold_in(part_splits[4], 1), 0, NF - 1).astype(jnp.int32)
    recv_data = gaussian(part_splits[5], (PAIRS, 2, RECV), 1.0, 6.0, ((0, 4),), jnp.float32)
    recv_weights = jnp.clip(jax.random.uniform(part_splits[6], (RECV, 64), jnp.float32, 0.05, 1.0), 0.05, 1.0)
    recv_x = place_ends(jax.random.randint(part_splits[7], (RECV,), 0, NX - 3), jax.random.fold_in(part_splits[7], 1), 0, (NX - 3) - 1).astype(jnp.int32)
    recv_y = place_ends(jax.random.randint(part_splits[8], (RECV,), 0, NY - 3), jax.random.fold_in(part_splits[8], 1), 0, (NY - 3) - 1).astype(jnp.int32)
    recv_z = place_ends(jax.random.randint(part_splits[9], (RECV,), 0, NZ - 3), jax.random.fold_in(part_splits[9], 1), 0, (NZ - 3) - 1).astype(jnp.int32)
    return dict(forward_field=forward_field, adjoint_guess=adjoint_guess, conductivity=conductivity, freq_kappa=freq_kappa, pair_freq=pair_freq, recv_data=recv_data, recv_weights=recv_weights, recv_x=recv_x, recv_y=recv_y, recv_z=recv_z)


def half_sweep(field, source, coupling, denominator, update_mask):
    padded = jnp.pad(field, ((0, 0), (1, 1), (1, 1), (1, 1)))
    beside_all = padded[:, 2:, 1:-1, 1:-1] + padded[:, :-2, 1:-1, 1:-1]
    beside_all = beside_all + padded[:, 1:-1, 2:, 1:-1] + padded[:, 1:-1, :-2, 1:-1]
    beside_all = beside_all + padded[:, 1:-1, 1:-1, 2:] + padded[:, 1:-1, 1:-1, :-2]
    sums = source + beside_all
    real_part = (6.0 * sums[0] + coupling * sums[1]) / denominator
    imag_part = (6.0 * sums[1] - coupling * sums[0]) / denominator
    return jnp.where(update_mask[None], jnp.stack([real_part, imag_part]), field)


def reference(forward_field, adjoint_guess, conductivity, freq_kappa, pair_freq, recv_data, recv_weights, recv_x, recv_y, recv_z):
    offsets = jnp.arange(64, dtype=jnp.int32)
    cell_x = recv_x[:, None] + offsets[None, :] // 16
    cell_y = recv_y[:, None] + (offsets[None, :] // 4) % 4
    cell_z = recv_z[:, None] + offsets[None, :] % 4
    flat_index = ((cell_x * NY + cell_y) * NZ + cell_z).reshape(-1).astype(jnp.int32)
    grid_x = jnp.arange(NX, dtype=jnp.int32)[:, None, None]
    grid_y = jnp.arange(NY, dtype=jnp.int32)[None, :, None]
    grid_z = jnp.arange(NZ, dtype=jnp.int32)[None, None, :]
    colours = (grid_x + grid_y + grid_z) % 2

    def one_pair(total, items):
        forward, guess, residual, freq_index = items
        kappa = freq_kappa[freq_index]
        values = (residual[:, :, None] * recv_weights[None]).reshape(2, -1)
        source = jnp.zeros((2, NX * NY * NZ), jnp.float32).at[:, flat_index].add(values).reshape(2, NX, NY, NZ)
        coupling = kappa * conductivity
        denominator = 36.0 + coupling * coupling
        field = guess
        for colour in (0, 1, 0, 1):
            field = half_sweep(field, source, coupling, denominator, colours == colour)
        total = total + kappa * (forward[0] * field[1] + forward[1] * field[0])
        return total, field

    total, adjoint = lax.scan(one_pair, jnp.zeros((NX, NY, NZ), jnp.float32), (forward_field, adjoint_guess, recv_data, pair_freq))
    return adjoint, -conductivity * total
```

```python
import functools

import jax
import jax.numpy as jnp
from jax import lax
from jax.experimental import pallas as pl
from jax.experimental.pallas import tpu as pltpu
from jax.sharding import PartitionSpec as P

MESH = pl.DeviceIdType.MESH
PAD = 8
F32 = jnp.float32
BF16 = jnp.bfloat16


def kernel(
    tiles,
    srcs,
    freq_ref,
    kappa_ref,
    fwd_hbm,
    guess_hbm,
    cond_hbm,
    data_ref,
    weights_ref,
    rx_ref,
    ry_ref,
    rz_ref,
    adj_ref,
    grad_ref,
    guess_ref,
    fwd_ref,
    cond_ref,
    b0_ref,
    r1_ref,
    b2_ref,
    r3_ref,
    halo_ref,
    src_ref,
    c6_ref,
    cc_ref,
    rows_ref,
    cols_ref,
    g_red,
    g_in,
    g_out,
    got_red,
    got_in,
    got_out,
    load_sem,
    send_sem,
    recv_sem,
    gsend_sem,
    grecv_sem,
):
    layers, _, half, size_z = src_ref.shape[1:]
    recv_count = rx_ref.shape[1]
    chunk = half // srcs
    last = layers - 1
    tile = lax.axis_index("tile")
    me = lax.axis_index("src")
    has_left = tile > 0
    has_right = tile < tiles - 1
    left = jnp.maximum(tile - 1, 0)
    right = jnp.minimum(tile + 1, tiles - 1)
    first_x = tile * layers

    loads = []

    def load(source, target):
        copy = pltpu.make_async_copy(source, target, load_sem.at[len(loads)])
        copy.start()
        loads.append(copy)
        return copy

    edge_loads = [load(guess_hbm.at[0, :, l], guess_ref.at[:, l]) for l in (0, last)]
    cond_load = load(cond_hbm, cond_ref)
    inner_load = load(guess_hbm.at[0, :, pl.ds(1, layers - 2)], guess_ref.at[:, pl.ds(1, layers - 2)])
    fwd_load = load(fwd_hbm.at[0], fwd_ref)

    barrier = pltpu.get_barrier_semaphore()

    @pl.when(has_left)
    def _():
        pl.semaphore_signal(barrier, inc=1, device_id={"tile": left}, device_id_type=MESH)

    @pl.when(has_right)
    def _():
        pl.semaphore_signal(barrier, inc=1, device_id={"tile": right}, device_id_type=MESH)

    for step in range(1, srcs):
        pl.semaphore_signal(
            barrier, inc=1, device_id={"src": lax.rem(me + step, srcs)}, device_id_type=MESH
        )

    lane = lax.broadcasted_iota(jnp.int32, (1, size_z), 1)

    def red_odd(l):
        return ((lane + (first_x + l)) & 1) == 1

    zeros_edge = jnp.zeros((PAD, size_z), F32)
    for buf in (b0_ref, r1_ref, b2_ref, r3_ref):
        for l in range(layers):
            for c in range(2):
                buf[l, c, 0:PAD, :] = zeros_edge
                buf[l, c, PAD + half : 2 * PAD + half, :] = zeros_edge

    @pl.when(jnp.logical_not(has_left))
    def _():
        for h in range(4):
            halo_ref[h, 0] = jnp.zeros((2, half, size_z), F32)

    @pl.when(jnp.logical_not(has_right))
    def _():
        for h in range(4):
            halo_ref[h, 1] = jnp.zeros((2, half, size_z), F32)

    even = pl.ds(0, half, stride=2)
    odd = pl.ds(1, half, stride=2)

    def pack_guess(l):
        pi = red_odd(l)
        for c in range(2):
            b0_ref[l, c, PAD : PAD + half, :] = jnp.where(
                pi, guess_ref[c, l, even, :], guess_ref[c, l, odd, :]
            )

    def halo_copy(h, buf, side):
        l, to = (last, right) if side == 0 else (0, left)
        return pltpu.make_async_remote_copy(
            src_ref=buf.at[l, :, pl.ds(PAD, half), :],
            dst_ref=halo_ref.at[h, side],
            send_sem=send_sem.at[h, side],
            recv_sem=recv_sem.at[h, side],
            device_id={"tile": to},
            device_id_type=MESH,
        )

    def halo_start(h, buf, side):
        @pl.when(has_right if side == 0 else has_left)
        def _():
            halo_copy(h, buf, side).start()

    def halo_wait(h, buf, side):
        @pl.when(has_left if side == 0 else has_right)
        def _():
            halo_copy(h, buf, side).wait_recv()

    def halo_sent(h, buf, side):
        @pl.when(has_right if side == 0 else has_left)
        def _():
            halo_copy(h, buf, side).wait_send()

    for copy, l in zip(edge_loads, (0, last)):
        copy.wait()
        pack_guess(l)

    peers = has_left.astype(jnp.int32) + has_right.astype(jnp.int32) + (srcs - 1)
    pl.semaphore_wait(barrier, peers)

    for side in range(2):
        halo_start(0, b0_ref, side)

    cond_load.wait()
    freq = freq_ref[0]
    kappa = jnp.float32(0.0)
    for i in range(kappa_ref.shape[0]):
        kappa = kappa + jnp.where(freq == i, kappa_ref[i], jnp.float32(0.0))
    for l in range(layers):
        pi = red_odd(l)
        ce = cond_ref[l, even, :]
        co = cond_ref[l, odd, :]
        for k, cell in enumerate((jnp.where(pi, co, ce), jnp.where(pi, ce, co))):
            coupling = kappa * cell
            inverse = 1.0 / (36.0 + coupling * coupling)
            c6_ref[k, l] = 6.0 * inverse
            cc_ref[k, l] = coupling * inverse
    inner_load.wait()
    for l in range(1, last):
        pack_guess(l)

    ry = ry_ref[...]
    row = lax.broadcasted_iota(jnp.int32, (half, recv_count), 0) * 2
    for parity in range(2):
        for b in range(4):
            rows_ref[parity * half : (parity + 1) * half, b * recv_count : (b + 1) * recv_count] = (
                jnp.where(row + parity == ry + b, 1.0, 0.0).astype(BF16)
            )
    w_t = jnp.transpose(weights_ref[...])
    rx = rx_ref[...]
    rz = rz_ref[...]
    ZC = 16
    for l in range(layers):
        pi = red_odd(l)
        at = (first_x + l) - rx
        plane = jnp.zeros((16, recv_count), F32)
        for a in range(4):
            plane = jnp.where(at == a, w_t[16 * a : 16 * a + 16, :], plane)
        for c in range(2):
            vals = plane * data_ref[c : c + 1, :]
            for z0 in range(0, size_z, ZC):
                off = lax.broadcasted_iota(jnp.int32, (ZC, recv_count), 0) + z0 - rz
                for b in range(4):
                    t = jnp.zeros((ZC, recv_count), F32)
                    for k in range(4):
                        t = jnp.where(off == k, vals[4 * b + k : 4 * b + k + 1, :], t)
                    hi = t.astype(BF16)
                    lo = (t - hi.astype(F32)).astype(BF16)
                    cols = slice(b * recv_count, (b + 1) * recv_count)
                    cols_ref[c, z0 : z0 + ZC, cols] = hi
                    cols_ref[c, size_z + z0 : size_z + z0 + ZC, cols] = lo
            both = lax.dot_general(
                rows_ref[...],
                cols_ref[c],
                (((1,), (1,)), ((), ())),
                preferred_element_type=F32,
            )
            total = both[:, :size_z] + both[:, size_z:]
            se, so = total[:half], total[half:]
            src_ref[0, l, c] = jnp.where(pi, so, se)
            src_ref[1, l, c] = jnp.where(pi, se, so)

    RC = min(32, half)

    def update(colour, h, buf, out, out_pad, l):
        up_side = red_odd(l) if colour == 0 else jnp.logical_not(red_odd(l))
        for r in range(0, half, RC):
            sums = []
            for c in range(2):
                mid = buf[l, c, PAD + r : PAD + r + RC, :]
                s = src_ref[colour, l, c, r : r + RC, :] + mid
                s = s + jnp.where(
                    up_side,
                    buf[l, c, PAD + r + 1 : PAD + r + 1 + RC, :],
                    buf[l, c, PAD + r - 1 : PAD + r - 1 + RC, :],
                )
                if l == 0:
                    s = s + halo_ref[h, 0, c, r : r + RC, :]
                else:
                    s = s + buf[l - 1, c, PAD + r : PAD + r + RC, :]
                if l == last:
                    s = s + halo_ref[h, 1, c, r : r + RC, :]
                else:
                    s = s + buf[l + 1, c, PAD + r : PAD + r + RC, :]
                s = s + jnp.where(lane == 0, 0.0, pltpu.roll(mid, 1, 1))
                s = s + jnp.where(lane == size_z - 1, 0.0, pltpu.roll(mid, size_z - 1, 1))
                sums.append(s)
            c6 = c6_ref[colour, l, r : r + RC, :]
            cc = cc_ref[colour, l, r : r + RC, :]
            out[l, 0, out_pad + r : out_pad + r + RC, :] = c6 * sums[0] + cc * sums[1]
            out[l, 1, out_pad + r : out_pad + r + RC, :] = c6 * sums[1] - cc * sums[0]

    def sweep(colour, h, buf, out):
        for l in range(1, last):
            update(colour, h, buf, out, PAD, l)
        for side in range(2):
            halo_wait(h, buf, side)
        update(colour, h, buf, out, PAD, last)
        if h < 3:
            halo_start(h + 1, out, 0)
        update(colour, h, buf, out, PAD, 0)
        if h < 3:
            halo_start(h + 1, out, 1)

    sweep(0, 0, b0_ref, r1_ref)
    sweep(1, 1, r1_ref, b2_ref)
    sweep(0, 2, b2_ref, r3_ref)

    def terms(colour, buf, out, l, slot):
        pi = red_odd(l) if colour == 0 else jnp.logical_not(red_odd(l))
        for s in range(srcs):
            e = pl.ds(2 * s * chunk, chunk, stride=2)
            o = pl.ds(2 * s * chunk + 1, chunk, stride=2)
            fre = jnp.where(pi, fwd_ref[0, l, o, :], fwd_ref[0, l, e, :])
            fim = jnp.where(pi, fwd_ref[1, l, o, :], fwd_ref[1, l, e, :])
            cell = jnp.where(pi, cond_ref[l, o, :], cond_ref[l, e, :])
            rows = pl.ds(PAD + s * chunk, chunk)
            value = fre * buf[l, 1, rows, :] + fim * buf[l, 0, rows, :]
            out[s, slot] = (-kappa * cell) * value

    def grad_copies(group, terms_ref, got_ref):
        copies = []
        for step in range(1, srcs):
            to = lax.rem(me + step, srcs)
            copies.append(
                pltpu.make_async_remote_copy(
                    src_ref=terms_ref.at[to],
                    dst_ref=got_ref.at[step - 1],
                    send_sem=gsend_sem.at[group, step - 1],
                    recv_sem=grecv_sem.at[group, step - 1],
                    device_id={"src": to},
                    device_id_type=MESH,
                )
            )
        return copies

    fwd_load.wait()
    for l in range(layers):
        terms(0, r3_ref, g_red, l, l)
    red_copies = grad_copies(0, g_red, got_red)
    for copy in red_copies:
        copy.start()

    def emit(l):
        pi = red_odd(l)
        for c in range(2):
            red = r3_ref[l, c, PAD : PAD + half, :]
            black = b0_ref[l, c, PAD : PAD + half, :]
            adj_ref[0, c, l, even, :] = jnp.where(pi, black, red)
            adj_ref[0, c, l, odd, :] = jnp.where(pi, red, black)

    for side in range(2):
        halo_sent(0, b0_ref, side)
    for l in range(1, last):
        update(1, 3, r3_ref, b0_ref, PAD, l)
        terms(1, b0_ref, g_in, l, l - 1)
    in_copies = grad_copies(1, g_in, got_in)
    for copy in in_copies:
        copy.start()
    for l in range(1, last):
        emit(l)
    for side in range(2):
        halo_wait(3, r3_ref, side)
    for slot, l in enumerate((0, last)):
        update(1, 3, r3_ref, b0_ref, PAD, l)
        terms(1, b0_ref, g_out, l, slot)
    out_copies = grad_copies(2, g_out, got_out)
    for copy in out_copies:
        copy.start()
    for l in (0, last):
        emit(l)

    for h, buf in ((1, r1_ref), (2, b2_ref), (3, r3_ref)):
        for side in range(2):
            halo_sent(h, buf, side)

    def summed(terms_ref, got_ref, slot):
        value = terms_ref[me, slot]
        for step in range(srcs - 1):
            value = value + got_ref[step, slot]
        return value

    def finish(l, black_ref, got_black, slot):
        pi = red_odd(l)
        red = summed(g_red, got_red, l)
        black = summed(black_ref, got_black, slot)
        grad_ref[l, pl.ds(0, chunk, stride=2), :] = jnp.where(pi, black, red)
        grad_ref[l, pl.ds(1, chunk, stride=2), :] = jnp.where(pi, red, black)

    for copy in red_copies:
        copy.wait()
    for copy in in_copies:
        copy.wait()
    for l in range(1, last):
        finish(l, g_in, got_in, l - 1)
    for copy in out_copies:
        copy.wait()
    for slot, l in enumerate((0, last)):
        finish(l, g_out, got_out, slot)


def body(
    forward_field,
    adjoint_guess,
    conductivity,
    freq_kappa,
    pair_freq,
    recv_data,
    recv_weights,
    recv_x,
    recv_y,
    recv_z,
):
    pair_count, parts, layers, size_y, size_z = adjoint_guess.shape
    assert pair_count == 1
    tiles = lax.axis_size("tile")
    srcs = lax.axis_size("src")
    half = size_y // 2
    chunk = half // srcs
    recv_count = recv_x.shape[0]
    field = (layers, parts, half + 2 * PAD, size_z)
    coef = (2, layers, half, size_z)
    vmem = pl.BlockSpec(memory_space=pltpu.VMEM)
    smem = pl.BlockSpec(memory_space=pltpu.SMEM)
    hbm = pl.BlockSpec(memory_space=pl.ANY)

    def grads(count, depth):
        return pltpu.VMEM((count, depth, chunk, size_z), F32)

    return pl.pallas_call(
        functools.partial(kernel, tiles, srcs),
        out_shape=(
            jax.ShapeDtypeStruct(adjoint_guess.shape, F32),
            jax.ShapeDtypeStruct((layers, size_y // srcs, size_z), F32),
        ),
        in_specs=[smem, smem, hbm, hbm, hbm, vmem, vmem, vmem, vmem, vmem],
        out_specs=(vmem, vmem),
        scratch_shapes=[
            pltpu.VMEM((parts, layers, size_y, size_z), F32),
            pltpu.VMEM((parts, layers, size_y, size_z), F32),
            pltpu.VMEM((layers, size_y, size_z), F32),
            pltpu.VMEM(field, F32),
            pltpu.VMEM(field, F32),
            pltpu.VMEM(field, F32),
            pltpu.VMEM(field, F32),
            pltpu.VMEM((4, 2, parts, half, size_z), F32),
            pltpu.VMEM((2, layers, parts, half, size_z), F32),
            pltpu.VMEM(coef, F32),
            pltpu.VMEM(coef, F32),
            pltpu.VMEM((size_y, 4 * recv_count), BF16),
            pltpu.VMEM((2, 2 * size_z, 4 * recv_count), BF16),
            grads(srcs, layers),
            grads(srcs, layers - 2),
            grads(srcs, 2),
            grads(srcs - 1, layers),
            grads(srcs - 1, layers - 2),
            grads(srcs - 1, 2),
            pltpu.SemaphoreType.DMA((5,)),
            pltpu.SemaphoreType.DMA((4, 2)),
            pltpu.SemaphoreType.DMA((4, 2)),
            pltpu.SemaphoreType.DMA((3, srcs - 1)),
            pltpu.SemaphoreType.DMA((3, srcs - 1)),
        ],
        compiler_params=pltpu.CompilerParams(
            collective_id=0, has_side_effects=True, vmem_limit_bytes=40 << 20
        ),
    )(
        pair_freq,
        freq_kappa,
        forward_field,
        adjoint_guess,
        conductivity,
        recv_data[0],
        recv_weights,
        recv_x[None],
        recv_y[None],
        recv_z[None],
    )


def solution(mesh):
    placed = (
        P(("job", "src"), None, "tile", None, None),
        P(("job", "src"), None, "tile", None, None),
        P(("job", "tile"), None, None),
        P("job"),
        P(("job", "src")),
        P(("job", "src"), None, None),
        P("job", None),
        P("job"),
        P("job"),
        P("job"),
    )
    return jax.shard_map(
        body,
        mesh=mesh,
        in_specs=placed,
        out_specs=(P(("job", "src"), None, "tile", None, None), P(("job", "tile"), "src", None)),
        check_vma=False,
    )
```

```python
import functools

import jax
import jax.numpy as jnp
from jax import lax
from jax.experimental import pallas as pl
from jax.experimental.pallas import tpu as pltpu
from jax.sharding import PartitionSpec as P

MESH = pl.DeviceIdType.MESH
PAD = 8
F32 = jnp.float32
BF16 = jnp.bfloat16


def kernel(
    tiles,
    srcs,
    freq_ref,
    kappa_ref,
    fwd_hbm,
    guess_hbm,
    cond_hbm,
    data_ref,
    weights_ref,
    rx_ref,
    ry_ref,
    rz_ref,
    adj_ref,
    grad_ref,
    guess_ref,
    fwd_ref,
    cond_ref,
    b0_ref,
    r1_ref,
    b2_ref,
    r3_ref,
    halo_ref,
    src_ref,
    c6_ref,
    cc_ref,
    rows_ref,
    cols_ref,
    g_red,
    g_in,
    g_out,
    got_red,
    got_in,
    got_out,
    load_sem,
    send_sem,
    recv_sem,
    gsend_sem,
    grecv_sem,
):
    layers, _, half, size_z = src_ref.shape[1:]
    recv_count = rx_ref.shape[1]
    chunk = half // srcs
    last = layers - 1
    tile = lax.axis_index("tile")
    me = lax.axis_index("src")
    has_left = tile > 0
    has_right = tile < tiles - 1
    left = jnp.maximum(tile - 1, 0)
    right = jnp.minimum(tile + 1, tiles - 1)
    first_x = tile * layers

    loads = []

    def load(source, target):
        copy = pltpu.make_async_copy(source, target, load_sem.at[len(loads)])
        copy.start()
        loads.append(copy)
        return copy

    edge_loads = [load(guess_hbm.at[0, :, l], guess_ref.at[:, l]) for l in (0, last)]
    cond_load = load(cond_hbm, cond_ref)
    inner_load = load(guess_hbm.at[0, :, pl.ds(1, layers - 2)], guess_ref.at[:, pl.ds(1, layers - 2)])
    fwd_load = load(fwd_hbm.at[0], fwd_ref)

    barrier = pltpu.get_barrier_semaphore()

    @pl.when(has_left)
    def _():
        pl.semaphore_signal(barrier, inc=1, device_id={"tile": left}, device_id_type=MESH)

    @pl.when(has_right)
    def _():
        pl.semaphore_signal(barrier, inc=1, device_id={"tile": right}, device_id_type=MESH)

    for step in range(1, srcs):
        pl.semaphore_signal(
            barrier, inc=1, device_id={"src": lax.rem(me + step, srcs)}, device_id_type=MESH
        )

    lane = lax.broadcasted_iota(jnp.int32, (1, size_z), 1)

    def red_odd(l):
        return ((lane + (first_x + l)) & 1) == 1

    zeros_edge = jnp.zeros((PAD, size_z), F32)
    for buf in (b0_ref, r1_ref, b2_ref, r3_ref):
        for l in range(layers):
            for c in range(2):
                buf[l, c, 0:PAD, :] = zeros_edge
                buf[l, c, PAD + half : 2 * PAD + half, :] = zeros_edge

    @pl.when(jnp.logical_not(has_left))
    def _():
        for h in range(4):
            halo_ref[h, 0] = jnp.zeros((2, half, size_z), F32)

    @pl.when(jnp.logical_not(has_right))
    def _():
        for h in range(4):
            halo_ref[h, 1] = jnp.zeros((2, half, size_z), F32)

    even = pl.ds(0, half, stride=2)
    odd = pl.ds(1, half, stride=2)

    def pack_guess(l):
        pi = red_odd(l)
        for c in range(2):
            b0_ref[l, c, PAD : PAD + half, :] = jnp.where(
                pi, guess_ref[c, l, even, :], guess_ref[c, l, odd, :]
            )

    def halo_copy(h, buf, side, s):
        l, to = (last, right) if side == 0 else (0, left)
        return pltpu.make_async_remote_copy(
            src_ref=buf.at[l, :, pl.ds(PAD + s * chunk, chunk), :],
            dst_ref=halo_ref.at[h, side, :, pl.ds(s * chunk, chunk), :],
            send_sem=send_sem.at[h, side, s],
            recv_sem=recv_sem.at[h, side, s],
            device_id={"tile": to},
            device_id_type=MESH,
        )

    def halo_start(h, buf, side, s):
        @pl.when(has_right if side == 0 else has_left)
        def _():
            halo_copy(h, buf, side, s).start()

    def halo_wait(h, buf, side, s):
        @pl.when(has_left if side == 0 else has_right)
        def _():
            halo_copy(h, buf, side, s).wait_recv()

    def halo_sent(h, buf, side):
        @pl.when(has_right if side == 0 else has_left)
        def _():
            for s in range(srcs):
                halo_copy(h, buf, side, s).wait_send()

    for copy, l in zip(edge_loads, (0, last)):
        copy.wait()
        pack_guess(l)

    peers = has_left.astype(jnp.int32) + has_right.astype(jnp.int32) + (srcs - 1)
    pl.semaphore_wait(barrier, peers)

    for s in range(srcs):
        for side in range(2):
            halo_start(0, b0_ref, side, s)

    cond_load.wait()
    freq = freq_ref[0]
    kappa = jnp.float32(0.0)
    for i in range(kappa_ref.shape[0]):
        kappa = kappa + jnp.where(freq == i, kappa_ref[i], jnp.float32(0.0))
    for l in range(layers):
        pi = red_odd(l)
        ce = cond_ref[l, even, :]
        co = cond_ref[l, odd, :]
        for k, cell in enumerate((jnp.where(pi, co, ce), jnp.where(pi, ce, co))):
            coupling = kappa * cell
            inverse = 1.0 / (36.0 + coupling * coupling)
            c6_ref[k, l] = 6.0 * inverse
            cc_ref[k, l] = coupling * inverse
    inner_load.wait()
    for l in range(1, last):
        pack_guess(l)

    ry = ry_ref[...]
    row = lax.broadcasted_iota(jnp.int32, (half, recv_count), 0) * 2
    for parity in range(2):
        for b in range(4):
            rows_ref[parity * half : (parity + 1) * half, b * recv_count : (b + 1) * recv_count] = (
                jnp.where(row + parity == ry + b, 1.0, 0.0).astype(BF16)
            )
    w_t = weights_ref[...]
    rx = rx_ref[...]
    rz = rz_ref[...]
    ZC = 16
    for l in range(layers):
        pi = red_odd(l)
        at = (first_x + l) - rx
        plane = jnp.zeros((16, recv_count), F32)
        for a in range(4):
            plane = jnp.where(at == a, w_t[16 * a : 16 * a + 16, :], plane)
        for c in range(2):
            vals = plane * data_ref[c : c + 1, :]
            for z0 in range(0, size_z, ZC):
                off = lax.broadcasted_iota(jnp.int32, (ZC, recv_count), 0) + z0 - rz
                for b in range(4):
                    t = jnp.zeros((ZC, recv_count), F32)
                    for k in range(4):
                        t = jnp.where(off == k, vals[4 * b + k : 4 * b + k + 1, :], t)
                    hi = t.astype(BF16)
                    lo = (t - hi.astype(F32)).astype(BF16)
                    cols = slice(b * recv_count, (b + 1) * recv_count)
                    cols_ref[c, z0 : z0 + ZC, cols] = hi
                    cols_ref[c, size_z + z0 : size_z + z0 + ZC, cols] = lo
            both = lax.dot_general(
                rows_ref[...],
                cols_ref[c],
                (((1,), (1,)), ((), ())),
                preferred_element_type=F32,
            )
            total = both[:, :size_z] + both[:, size_z:]
            se, so = total[:half], total[half:]
            src_ref[0, l, c] = jnp.where(pi, so, se)
            src_ref[1, l, c] = jnp.where(pi, se, so)

    def update(colour, h, buf, out, out_pad, l, pieces):
        up_side = red_odd(l) if colour == 0 else jnp.logical_not(red_odd(l))
        for r in (chunk * s for s in pieces):
            sums = []
            for c in range(2):
                mid = buf[l, c, PAD + r : PAD + r + chunk, :]
                s = src_ref[colour, l, c, r : r + chunk, :] + mid
                s = s + jnp.where(
                    up_side,
                    buf[l, c, PAD + r + 1 : PAD + r + 1 + chunk, :],
                    buf[l, c, PAD + r - 1 : PAD + r - 1 + chunk, :],
                )
                if l == 0:
                    s = s + halo_ref[h, 0, c, r : r + chunk, :]
                else:
                    s = s + buf[l - 1, c, PAD + r : PAD + r + chunk, :]
                if l == last:
                    s = s + halo_ref[h, 1, c, r : r + chunk, :]
                else:
                    s = s + buf[l + 1, c, PAD + r : PAD + r + chunk, :]
                s = s + jnp.where(lane == 0, 0.0, pltpu.roll(mid, 1, 1))
                s = s + jnp.where(lane == size_z - 1, 0.0, pltpu.roll(mid, size_z - 1, 1))
                sums.append(s)
            c6 = c6_ref[colour, l, r : r + chunk, :]
            cc = cc_ref[colour, l, r : r + chunk, :]
            out[l, 0, out_pad + r : out_pad + r + chunk, :] = c6 * sums[0] + cc * sums[1]
            out[l, 1, out_pad + r : out_pad + r + chunk, :] = c6 * sums[1] - cc * sums[0]

    every = range(srcs)

    def sweep(colour, h, buf, out):
        for l in range(1, last):
            update(colour, h, buf, out, PAD, l, every)
        for s in every:
            for side, l in ((0, 0), (1, last)):
                halo_wait(h, buf, side, s)
                update(colour, h, buf, out, PAD, l, (s,))
                halo_start(h + 1, out, 1 - side, s)

    sweep(0, 0, b0_ref, r1_ref)
    sweep(1, 1, r1_ref, b2_ref)
    sweep(0, 2, b2_ref, r3_ref)

    def terms(colour, buf, out, l, slot, pieces):
        pi = red_odd(l) if colour == 0 else jnp.logical_not(red_odd(l))
        for s in pieces:
            e = pl.ds(2 * s * chunk, chunk, stride=2)
            o = pl.ds(2 * s * chunk + 1, chunk, stride=2)
            fre = jnp.where(pi, fwd_ref[0, l, o, :], fwd_ref[0, l, e, :])
            fim = jnp.where(pi, fwd_ref[1, l, o, :], fwd_ref[1, l, e, :])
            cell = jnp.where(pi, cond_ref[l, o, :], cond_ref[l, e, :])
            rows = pl.ds(PAD + s * chunk, chunk)
            value = fre * buf[l, 1, rows, :] + fim * buf[l, 0, rows, :]
            out[s, slot] = (-kappa * cell) * value

    def grad_copies(group, terms_ref, got_ref):
        copies = []
        for step in range(1, srcs):
            to = lax.rem(me + step, srcs)
            copies.append(
                pltpu.make_async_remote_copy(
                    src_ref=terms_ref.at[to],
                    dst_ref=got_ref.at[step - 1],
                    send_sem=gsend_sem.at[group, step - 1],
                    recv_sem=grecv_sem.at[group, step - 1],
                    device_id={"src": to},
                    device_id_type=MESH,
                )
            )
        return copies

    fwd_load.wait()
    for l in range(layers):
        terms(0, r3_ref, g_red, l, l, every)
    red_copies = grad_copies(0, g_red, got_red)
    for copy in red_copies:
        copy.start()

    def emit(l):
        pi = red_odd(l)
        for c in range(2):
            red = r3_ref[l, c, PAD : PAD + half, :]
            black = b0_ref[l, c, PAD : PAD + half, :]
            adj_ref[0, c, l, even, :] = jnp.where(pi, black, red)
            adj_ref[0, c, l, odd, :] = jnp.where(pi, red, black)

    for side in range(2):
        halo_sent(0, b0_ref, side)
    for l in range(1, last):
        update(1, 3, r3_ref, b0_ref, PAD, l, every)
        terms(1, b0_ref, g_in, l, l - 1, every)
    in_copies = grad_copies(1, g_in, got_in)
    for copy in in_copies:
        copy.start()
    for l in range(1, last):
        emit(l)
    def out_copy(s):
        step = lax.rem(s - me + srcs - 1, srcs)
        return pltpu.make_async_remote_copy(
            src_ref=g_out.at[s],
            dst_ref=got_out.at[step],
            send_sem=gsend_sem.at[2, step],
            recv_sem=grecv_sem.at[2, step],
            device_id={"src": s},
            device_id_type=MESH,
        )

    for s in every:
        for side, l in ((0, 0), (1, last)):
            halo_wait(3, r3_ref, side, s)
            update(1, 3, r3_ref, b0_ref, PAD, l, (s,))
            terms(1, b0_ref, g_out, l, side, (s,))

        @pl.when(me != s)
        def _():
            out_copy(s).start()

    out_copies = grad_copies(2, g_out, got_out)
    for l in (0, last):
        emit(l)

    for h, buf in ((1, r1_ref), (2, b2_ref), (3, r3_ref)):
        for side in range(2):
            halo_sent(h, buf, side)

    def summed(terms_ref, got_ref, slot):
        value = terms_ref[me, slot]
        for step in range(srcs - 1):
            value = value + got_ref[step, slot]
        return value

    def finish(l, black_ref, got_black, slot):
        pi = red_odd(l)
        red = summed(g_red, got_red, l)
        black = summed(black_ref, got_black, slot)
        grad_ref[l, pl.ds(0, chunk, stride=2), :] = jnp.where(pi, black, red)
        grad_ref[l, pl.ds(1, chunk, stride=2), :] = jnp.where(pi, red, black)

    for copy in red_copies:
        copy.wait()
    for copy in in_copies:
        copy.wait()
    for l in range(1, last):
        finish(l, g_in, got_in, l - 1)
    for copy in out_copies:
        copy.wait()
    for slot, l in enumerate((0, last)):
        finish(l, g_out, got_out, slot)


def body(
    forward_field,
    adjoint_guess,
    conductivity,
    freq_kappa,
    pair_freq,
    recv_data,
    recv_weights,
    recv_x,
    recv_y,
    recv_z,
):
    pair_count, parts, layers, size_y, size_z = adjoint_guess.shape
    assert pair_count == 1
    tiles = lax.axis_size("tile")
    srcs = lax.axis_size("src")
    half = size_y // 2
    chunk = half // srcs
    recv_count = recv_x.shape[0]
    field = (layers, parts, half + 2 * PAD, size_z)
    coef = (2, layers, half, size_z)
    vmem = pl.BlockSpec(memory_space=pltpu.VMEM)
    smem = pl.BlockSpec(memory_space=pltpu.SMEM)
    hbm = pl.BlockSpec(memory_space=pltpu.HBM)

    def grads(count, depth):
        return pltpu.VMEM((count, depth, chunk, size_z), F32)

    results = pl.pallas_call(
        functools.partial(kernel, tiles, srcs),
        out_shape=(
            jax.ShapeDtypeStruct(adjoint_guess.shape, F32),
            jax.ShapeDtypeStruct((layers, size_y // srcs, size_z), F32),
        ),
        in_specs=[smem, smem, hbm, hbm, hbm, vmem, vmem, vmem, vmem, vmem],
        out_specs=(vmem, vmem),
        scratch_shapes=[
            pltpu.VMEM((parts, layers, size_y, size_z), F32),
            pltpu.VMEM((parts, layers, size_y, size_z), F32),
            pltpu.VMEM((layers, size_y, size_z), F32),
            pltpu.VMEM(field, F32),
            pltpu.VMEM(field, F32),
            pltpu.VMEM(field, F32),
            pltpu.VMEM(field, F32),
            pltpu.VMEM((4, 2, parts, half, size_z), F32),
            pltpu.VMEM((2, layers, parts, half, size_z), F32),
            pltpu.VMEM(coef, F32),
            pltpu.VMEM(coef, F32),
            pltpu.VMEM((size_y, 4 * recv_count), BF16),
            pltpu.VMEM((2, 2 * size_z, 4 * recv_count), BF16),
            grads(srcs, layers),
            grads(srcs, layers - 2),
            grads(srcs, 2),
            grads(srcs - 1, layers),
            grads(srcs - 1, layers - 2),
            grads(srcs - 1, 2),
            pltpu.SemaphoreType.DMA((5,)),
            pltpu.SemaphoreType.DMA((4, 2, srcs)),
            pltpu.SemaphoreType.DMA((4, 2, srcs)),
            pltpu.SemaphoreType.DMA((3, srcs - 1)),
            pltpu.SemaphoreType.DMA((3, srcs - 1)),
        ],
        compiler_params=pltpu.CompilerParams(
            collective_id=0, has_side_effects=True, vmem_limit_bytes=58 << 20
        ),
    )(
        pair_freq,
        freq_kappa,
        forward_field,
        adjoint_guess,
        conductivity,
        recv_data[0],
        recv_weights.T,
        recv_x[None],
        recv_y[None],
        recv_z[None],
    )
    return results


def solution(mesh):
    placed = (
        P(("job", "src"), None, "tile", None, None),
        P(("job", "src"), None, "tile", None, None),
        P(("job", "tile"), None, None),
        P("job"),
        P(("job", "src")),
        P(("job", "src"), None, None),
        P("job", None),
        P("job"),
        P("job"),
        P("job"),
    )
    return jax.shard_map(
        body,
        mesh=mesh,
        in_specs=placed,
        out_specs=(P(("job", "src"), None, "tile", None, None), P(("job", "tile"), "src", None)),
        check_vma=False,
    )
```

```python
import functools

import jax
import jax.numpy as jnp
from jax import lax
from jax.experimental import pallas as pl
from jax.experimental.pallas import tpu as pltpu
from jax.sharding import PartitionSpec as P

MESH = pl.DeviceIdType.MESH
PAD = 8
F32 = jnp.float32
BF16 = jnp.bfloat16


def kernel(
    tiles,
    srcs,
    freq_ref,
    kappa_ref,
    fwd_hbm,
    guess_hbm,
    cond_hbm,
    data_ref,
    weights_ref,
    rx_ref,
    ry_ref,
    rz_ref,
    adj_ref,
    grad_ref,
    guess_ref,
    fwd_ref,
    cond_ref,
    b0_ref,
    r1_ref,
    b2_ref,
    r3_ref,
    halo_ref,
    src_ref,
    c6_ref,
    cc_ref,
    rows_ref,
    cols_ref,
    g_red,
    g_rim,
    g_in,
    g_out,
    got_red,
    got_rim,
    got_in,
    got_out,
    load_sem,
    send_sem,
    recv_sem,
    gsend_sem,
    grecv_sem,
):
    layers, _, half, size_z = src_ref.shape[1:]
    recv_count = rx_ref.shape[1]
    chunk = half // srcs
    last = layers - 1
    tile = lax.axis_index("tile")
    me = lax.axis_index("src")
    has_left = tile > 0
    has_right = tile < tiles - 1
    left = jnp.maximum(tile - 1, 0)
    right = jnp.minimum(tile + 1, tiles - 1)
    first_x = tile * layers

    loads = []

    def load(source, target):
        copy = pltpu.make_async_copy(source, target, load_sem.at[len(loads)])
        copy.start()
        loads.append(copy)
        return copy

    edge_loads = [load(guess_hbm.at[0, :, l], guess_ref.at[:, l]) for l in (0, last)]
    cond_load = load(cond_hbm, cond_ref)
    inner_load = load(guess_hbm.at[0, :, pl.ds(1, layers - 2)], guess_ref.at[:, pl.ds(1, layers - 2)])
    fwd_load = load(fwd_hbm.at[0], fwd_ref)

    barrier = pltpu.get_barrier_semaphore()

    @pl.when(has_left)
    def _():
        pl.semaphore_signal(barrier, inc=1, device_id={"tile": left}, device_id_type=MESH)

    @pl.when(has_right)
    def _():
        pl.semaphore_signal(barrier, inc=1, device_id={"tile": right}, device_id_type=MESH)

    for step in range(1, srcs):
        pl.semaphore_signal(
            barrier, inc=1, device_id={"src": lax.rem(me + step, srcs)}, device_id_type=MESH
        )

    lane = lax.broadcasted_iota(jnp.int32, (1, size_z), 1)

    def red_odd(l):
        return ((lane + (first_x + l)) & 1) == 1

    zeros_edge = jnp.zeros((PAD, size_z), F32)
    for buf in (b0_ref, r1_ref, b2_ref, r3_ref):
        for l in range(layers):
            for c in range(2):
                buf[l, c, 0:PAD, :] = zeros_edge
                buf[l, c, PAD + half : 2 * PAD + half, :] = zeros_edge

    @pl.when(jnp.logical_not(has_left))
    def _():
        for h in range(4):
            halo_ref[h, 0] = jnp.zeros((2, half, size_z), F32)

    @pl.when(jnp.logical_not(has_right))
    def _():
        for h in range(4):
            halo_ref[h, 1] = jnp.zeros((2, half, size_z), F32)

    even = pl.ds(0, half, stride=2)
    odd = pl.ds(1, half, stride=2)

    def pack_guess(l):
        pi = red_odd(l)
        for c in range(2):
            b0_ref[l, c, PAD : PAD + half, :] = jnp.where(
                pi, guess_ref[c, l, even, :], guess_ref[c, l, odd, :]
            )

    def halo_copy(h, buf, side, s):
        l, to = (last, right) if side == 0 else (0, left)
        return pltpu.make_async_remote_copy(
            src_ref=buf.at[l, :, pl.ds(PAD + s * chunk, chunk), :],
            dst_ref=halo_ref.at[h, side, :, pl.ds(s * chunk, chunk), :],
            send_sem=send_sem.at[h, side, s],
            recv_sem=recv_sem.at[h, side, s],
            device_id={"tile": to},
            device_id_type=MESH,
        )

    def halo_start(h, buf, side, s):
        @pl.when(has_right if side == 0 else has_left)
        def _():
            halo_copy(h, buf, side, s).start()

    def halo_wait(h, buf, side, s):
        @pl.when(has_left if side == 0 else has_right)
        def _():
            halo_copy(h, buf, side, s).wait_recv()

    def halo_sent(h, buf, side):
        @pl.when(has_right if side == 0 else has_left)
        def _():
            for s in range(srcs):
                halo_copy(h, buf, side, s).wait_send()

    for copy, l in zip(edge_loads, (0, last)):
        copy.wait()
        pack_guess(l)

    peers = has_left.astype(jnp.int32) + has_right.astype(jnp.int32) + (srcs - 1)
    pl.semaphore_wait(barrier, peers)

    for s in range(srcs):
        for side in range(2):
            halo_start(0, b0_ref, side, s)

    cond_load.wait()
    freq = freq_ref[0]
    kappa = jnp.float32(0.0)
    for i in range(kappa_ref.shape[0]):
        kappa = kappa + jnp.where(freq == i, kappa_ref[i], jnp.float32(0.0))
    for l in range(layers):
        pi = red_odd(l)
        ce = cond_ref[l, even, :]
        co = cond_ref[l, odd, :]
        for k, cell in enumerate((jnp.where(pi, co, ce), jnp.where(pi, ce, co))):
            coupling = kappa * cell
            inverse = 1.0 / (36.0 + coupling * coupling)
            c6_ref[k, l] = 6.0 * inverse
            cc_ref[k, l] = coupling * inverse
    inner_load.wait()
    for l in range(1, last):
        pack_guess(l)

    ry = ry_ref[...]
    row = lax.broadcasted_iota(jnp.int32, (half, recv_count), 0) * 2
    for parity in range(2):
        for b in range(4):
            rows_ref[parity * half : (parity + 1) * half, b * recv_count : (b + 1) * recv_count] = (
                jnp.where(row + parity == ry + b, 1.0, 0.0).astype(BF16)
            )
    w_t = weights_ref[...]
    rx = rx_ref[...]
    rz = rz_ref[...]
    ZC = 16
    for l in range(layers):
        pi = red_odd(l)
        at = (first_x + l) - rx
        plane = jnp.zeros((16, recv_count), F32)
        for a in range(4):
            plane = jnp.where(at == a, w_t[16 * a : 16 * a + 16, :], plane)
        for c in range(2):
            vals = plane * data_ref[c : c + 1, :]
            for z0 in range(0, size_z, ZC):
                off = lax.broadcasted_iota(jnp.int32, (ZC, recv_count), 0) + z0 - rz
                for b in range(4):
                    t = jnp.zeros((ZC, recv_count), F32)
                    for k in range(4):
                        t = jnp.where(off == k, vals[4 * b + k : 4 * b + k + 1, :], t)
                    hi = t.astype(BF16)
                    lo = (t - hi.astype(F32)).astype(BF16)
                    cols = slice(b * recv_count, (b + 1) * recv_count)
                    cols_ref[c, z0 : z0 + ZC, cols] = hi
                    cols_ref[c, size_z + z0 : size_z + z0 + ZC, cols] = lo
            both = lax.dot_general(
                rows_ref[...],
                cols_ref[c],
                (((1,), (1,)), ((), ())),
                preferred_element_type=F32,
            )
            total = both[:, :size_z] + both[:, size_z:]
            se, so = total[:half], total[half:]
            src_ref[0, l, c] = jnp.where(pi, so, se)
            src_ref[1, l, c] = jnp.where(pi, se, so)

    def update(colour, h, buf, out, out_pad, l, pieces):
        up_side = red_odd(l) if colour == 0 else jnp.logical_not(red_odd(l))
        for r in (chunk * s for s in pieces):
            sums = []
            for c in range(2):
                mid = buf[l, c, PAD + r : PAD + r + chunk, :]
                s = src_ref[colour, l, c, r : r + chunk, :] + mid
                s = s + jnp.where(
                    up_side,
                    buf[l, c, PAD + r + 1 : PAD + r + 1 + chunk, :],
                    buf[l, c, PAD + r - 1 : PAD + r - 1 + chunk, :],
                )
                if l == 0:
                    s = s + halo_ref[h, 0, c, r : r + chunk, :]
                else:
                    s = s + buf[l - 1, c, PAD + r : PAD + r + chunk, :]
                if l == last:
                    s = s + halo_ref[h, 1, c, r : r + chunk, :]
                else:
                    s = s + buf[l + 1, c, PAD + r : PAD + r + chunk, :]
                s = s + jnp.where(lane == 0, 0.0, pltpu.roll(mid, 1, 1))
                s = s + jnp.where(lane == size_z - 1, 0.0, pltpu.roll(mid, size_z - 1, 1))
                sums.append(s)
            c6 = c6_ref[colour, l, r : r + chunk, :]
            cc = cc_ref[colour, l, r : r + chunk, :]
            out[l, 0, out_pad + r : out_pad + r + chunk, :] = c6 * sums[0] + cc * sums[1]
            out[l, 1, out_pad + r : out_pad + r + chunk, :] = c6 * sums[1] - cc * sums[0]

    every = range(srcs)

    def sweep(colour, h, buf, out, between=lambda: None):
        for l in range(1, last):
            update(colour, h, buf, out, PAD, l, every)
        between()
        for s in every:
            for side, l in ((0, 0), (1, last)):
                halo_wait(h, buf, side, s)
                update(colour, h, buf, out, PAD, l, (s,))
                halo_start(h + 1, out, 1 - side, s)

    sweep(0, 0, b0_ref, r1_ref)
    sweep(1, 1, r1_ref, b2_ref)

    def terms(colour, buf, out, l, slot, pieces):
        pi = red_odd(l) if colour == 0 else jnp.logical_not(red_odd(l))
        for s in pieces:
            e = pl.ds(2 * s * chunk, chunk, stride=2)
            o = pl.ds(2 * s * chunk + 1, chunk, stride=2)
            fre = jnp.where(pi, fwd_ref[0, l, o, :], fwd_ref[0, l, e, :])
            fim = jnp.where(pi, fwd_ref[1, l, o, :], fwd_ref[1, l, e, :])
            cell = jnp.where(pi, cond_ref[l, o, :], cond_ref[l, e, :])
            rows = pl.ds(PAD + s * chunk, chunk)
            value = fre * buf[l, 1, rows, :] + fim * buf[l, 0, rows, :]
            out[s, slot] = (-kappa * cell) * value

    def grad_copies(group, terms_ref, got_ref):
        copies = []
        for step in range(1, srcs):
            to = lax.rem(me + step, srcs)
            copies.append(
                pltpu.make_async_remote_copy(
                    src_ref=terms_ref.at[to],
                    dst_ref=got_ref.at[step - 1],
                    send_sem=gsend_sem.at[group, step - 1],
                    recv_sem=grecv_sem.at[group, step - 1],
                    device_id={"src": to},
                    device_id_type=MESH,
                )
            )
        return copies

    red_copies = grad_copies(0, g_red, got_red)

    def red_inner():
        fwd_load.wait()
        for l in range(1, last):
            terms(0, r3_ref, g_red, l, l - 1, every)
        for copy in red_copies:
            copy.start()

    sweep(0, 2, b2_ref, r3_ref, red_inner)
    for slot, l in enumerate((0, last)):
        terms(0, r3_ref, g_rim, l, slot, every)
    rim_copies = grad_copies(3, g_rim, got_rim)
    for copy in rim_copies:
        copy.start()

    def emit(l):
        pi = red_odd(l)
        for c in range(2):
            red = r3_ref[l, c, PAD : PAD + half, :]
            black = b0_ref[l, c, PAD : PAD + half, :]
            adj_ref[0, c, l, even, :] = jnp.where(pi, black, red)
            adj_ref[0, c, l, odd, :] = jnp.where(pi, red, black)

    for side in range(2):
        halo_sent(0, b0_ref, side)
    for l in range(1, last):
        update(1, 3, r3_ref, b0_ref, PAD, l, every)
        terms(1, b0_ref, g_in, l, l - 1, every)
    in_copies = grad_copies(1, g_in, got_in)
    for copy in in_copies:
        copy.start()
    for l in range(1, last):
        emit(l)
    def out_copy(s):
        step = lax.rem(s - me + srcs - 1, srcs)
        return pltpu.make_async_remote_copy(
            src_ref=g_out.at[s],
            dst_ref=got_out.at[step],
            send_sem=gsend_sem.at[2, step],
            recv_sem=grecv_sem.at[2, step],
            device_id={"src": s},
            device_id_type=MESH,
        )

    for s in every:
        for side, l in ((0, 0), (1, last)):
            halo_wait(3, r3_ref, side, s)
            update(1, 3, r3_ref, b0_ref, PAD, l, (s,))
            terms(1, b0_ref, g_out, l, side, (s,))

        @pl.when(me != s)
        def _():
            out_copy(s).start()

    out_copies = grad_copies(2, g_out, got_out)
    for l in (0, last):
        emit(l)

    for h, buf in ((1, r1_ref), (2, b2_ref), (3, r3_ref)):
        for side in range(2):
            halo_sent(h, buf, side)

    def summed(terms_ref, got_ref, slot):
        value = terms_ref[me, slot]
        for step in range(srcs - 1):
            value = value + got_ref[step, slot]
        return value

    def finish(l, red_ref, got_red, black_ref, got_black, slot):
        pi = red_odd(l)
        red = summed(red_ref, got_red, slot)
        black = summed(black_ref, got_black, slot)
        grad_ref[l, pl.ds(0, chunk, stride=2), :] = jnp.where(pi, black, red)
        grad_ref[l, pl.ds(1, chunk, stride=2), :] = jnp.where(pi, red, black)

    for copy in red_copies:
        copy.wait()
    for copy in in_copies:
        copy.wait()
    for l in range(1, last):
        finish(l, g_red, got_red, g_in, got_in, l - 1)
    for copy in rim_copies:
        copy.wait()
    for copy in out_copies:
        copy.wait()
    for slot, l in enumerate((0, last)):
        finish(l, g_rim, got_rim, g_out, got_out, slot)


def store_kernel(adj_ref, grad_ref, adj_hbm, grad_hbm, sem):
    parts, layers = adj_ref.shape[1:3]
    copies = [pltpu.make_async_copy(grad_ref, grad_hbm, sem.at[0])]
    for c in range(parts):
        for l in range(layers):
            copies.append(
                pltpu.make_async_copy(adj_ref.at[0, c, l], adj_hbm.at[0, c, l], sem.at[len(copies)])
            )
    for copy in copies:
        copy.start()
    for copy in copies:
        copy.wait()


def body(
    forward_field,
    adjoint_guess,
    conductivity,
    freq_kappa,
    pair_freq,
    recv_data,
    recv_weights,
    recv_x,
    recv_y,
    recv_z,
):
    pair_count, parts, layers, size_y, size_z = adjoint_guess.shape
    assert pair_count == 1
    tiles = lax.axis_size("tile")
    srcs = lax.axis_size("src")
    half = size_y // 2
    chunk = half // srcs
    recv_count = recv_x.shape[0]
    field = (layers, parts, half + 2 * PAD, size_z)
    coef = (2, layers, half, size_z)
    vmem = pl.BlockSpec(memory_space=pltpu.VMEM)
    smem = pl.BlockSpec(memory_space=pltpu.SMEM)
    hbm = pl.BlockSpec(memory_space=pltpu.HBM)

    def grads(count, depth):
        return pltpu.VMEM((count, depth, chunk, size_z), F32)

    results = pl.pallas_call(
        functools.partial(kernel, tiles, srcs),
        out_shape=(
            jax.ShapeDtypeStruct(adjoint_guess.shape, F32),
            jax.ShapeDtypeStruct((layers, size_y // srcs, size_z), F32),
        ),
        in_specs=[smem, smem, hbm, hbm, hbm, vmem, vmem, vmem, vmem, vmem],
        out_specs=(vmem, vmem),
        scratch_shapes=[
            pltpu.VMEM((parts, layers, size_y, size_z), F32),
            pltpu.VMEM((parts, layers, size_y, size_z), F32),
            pltpu.VMEM((layers, size_y, size_z), F32),
            pltpu.VMEM(field, F32),
            pltpu.VMEM(field, F32),
            pltpu.VMEM(field, F32),
            pltpu.VMEM(field, F32),
            pltpu.VMEM((4, 2, parts, half, size_z), F32),
            pltpu.VMEM((2, layers, parts, half, size_z), F32),
            pltpu.VMEM(coef, F32),
            pltpu.VMEM(coef, F32),
            pltpu.VMEM((size_y, 4 * recv_count), BF16),
            pltpu.VMEM((2, 2 * size_z, 4 * recv_count), BF16),
            grads(srcs, layers - 2),
            grads(srcs, 2),
            grads(srcs, layers - 2),
            grads(srcs, 2),
            grads(srcs - 1, layers - 2),
            grads(srcs - 1, 2),
            grads(srcs - 1, layers - 2),
            grads(srcs - 1, 2),
            pltpu.SemaphoreType.DMA((5,)),
            pltpu.SemaphoreType.DMA((4, 2, srcs)),
            pltpu.SemaphoreType.DMA((4, 2, srcs)),
            pltpu.SemaphoreType.DMA((4, srcs - 1)),
            pltpu.SemaphoreType.DMA((4, srcs - 1)),
        ],
        compiler_params=pltpu.CompilerParams(
            collective_id=0, has_side_effects=True, vmem_limit_bytes=40 << 20
        ),
    )(
        pair_freq,
        freq_kappa,
        *(
            pltpu.with_memory_space_constraint(a, pltpu.HBM)
            for a in (forward_field, adjoint_guess, conductivity)
        ),
        recv_data[0],
        recv_weights.T,
        recv_x[None],
        recv_y[None],
        recv_z[None],
    )
    return pl.pallas_call(
        store_kernel,
        out_shape=tuple(jax.ShapeDtypeStruct(r.shape, F32) for r in results),
        in_specs=[vmem, vmem],
        out_specs=(hbm, hbm),
        scratch_shapes=[pltpu.SemaphoreType.DMA((1 + parts * layers,))],
        compiler_params=pltpu.CompilerParams(vmem_limit_bytes=2 << 20),
    )(*results)


def solution(mesh):
    placed = (
        P(("job", "src"), None, "tile", None, None),
        P(("job", "src"), None, "tile", None, None),
        P(("job", "tile"), None, None),
        P("job"),
        P(("job", "src")),
        P(("job", "src"), None, None),
        P("job", None),
        P("job"),
        P("job"),
        P("job"),
    )
    return jax.shard_map(
        body,
        mesh=mesh,
        in_specs=placed,
        out_specs=(P(("job", "src"), None, "tile", None, None), P(("job", "tile"), "src", None)),
        check_vma=False,
    )
```

```python
import functools

import jax
import jax.numpy as jnp
from jax import lax
from jax.experimental import pallas as pl
from jax.experimental.pallas import tpu as pltpu
from jax.sharding import PartitionSpec as P

MESH = pl.DeviceIdType.MESH
PAD = 8
F32 = jnp.float32
BF16 = jnp.bfloat16


def kernel(
    tiles,
    srcs,
    freq_ref,
    kappa_ref,
    fwd_hbm,
    guess_hbm,
    cond_hbm,
    data_ref,
    weights_ref,
    rx_ref,
    ry_ref,
    rz_ref,
    adj_ref,
    grad_ref,
    guess_ref,
    fwd_ref,
    cond_ref,
    b0_ref,
    r1_ref,
    b2_ref,
    r3_ref,
    halo_ref,
    src_ref,
    c6_ref,
    cc_ref,
    rows_ref,
    cols_ref,
    g_red,
    g_rim,
    g_in,
    g_out,
    got_red,
    got_rim,
    got_in,
    got_out,
    load_sem,
    send_sem,
    recv_sem,
    gsend_sem,
    grecv_sem,
):
    layers, _, half, size_z = src_ref.shape[1:]
    recv_count = rx_ref.shape[1]
    chunk = half // srcs
    last = layers - 1
    tile = lax.axis_index("tile")
    me = lax.axis_index("src")
    has_left = tile > 0
    has_right = tile < tiles - 1
    left = jnp.maximum(tile - 1, 0)
    right = jnp.minimum(tile + 1, tiles - 1)
    first_x = tile * layers

    loads = []

    def load(source, target):
        copy = pltpu.make_async_copy(source, target, load_sem.at[len(loads)])
        copy.start()
        loads.append(copy)
        return copy

    edge_loads = [load(guess_hbm.at[0, :, l], guess_ref.at[:, l]) for l in (0, last)]
    cond_load = load(cond_hbm, cond_ref)
    inner_load = load(guess_hbm.at[0, :, pl.ds(1, layers - 2)], guess_ref.at[:, pl.ds(1, layers - 2)])
    fwd_load = load(fwd_hbm.at[0], fwd_ref)

    barrier = pltpu.get_barrier_semaphore()

    @pl.when(has_left)
    def _():
        pl.semaphore_signal(barrier, inc=1, device_id={"tile": left}, device_id_type=MESH)

    @pl.when(has_right)
    def _():
        pl.semaphore_signal(barrier, inc=1, device_id={"tile": right}, device_id_type=MESH)

    for step in range(1, srcs):
        pl.semaphore_signal(
            barrier, inc=1, device_id={"src": lax.rem(me + step, srcs)}, device_id_type=MESH
        )

    lane = lax.broadcasted_iota(jnp.int32, (1, size_z), 1)

    def red_odd(l):
        return ((lane + (first_x + l)) & 1) == 1

    zeros_edge = jnp.zeros((PAD, size_z), F32)
    for buf in (b0_ref, r1_ref, b2_ref, r3_ref):
        for l in range(layers):
            for c in range(2):
                buf[l, c, 0:PAD, :] = zeros_edge
                buf[l, c, PAD + half : 2 * PAD + half, :] = zeros_edge

    @pl.when(jnp.logical_not(has_left))
    def _():
        for h in range(4):
            halo_ref[h, 0] = jnp.zeros((2, half, size_z), F32)

    @pl.when(jnp.logical_not(has_right))
    def _():
        for h in range(4):
            halo_ref[h, 1] = jnp.zeros((2, half, size_z), F32)

    even = pl.ds(0, half, stride=2)
    odd = pl.ds(1, half, stride=2)

    def pack_guess(l):
        pi = red_odd(l)
        for c in range(2):
            b0_ref[l, c, PAD : PAD + half, :] = jnp.where(
                pi, guess_ref[c, l, even, :], guess_ref[c, l, odd, :]
            )

    def halo_copy(h, buf, side, s):
        l, to = (last, right) if side == 0 else (0, left)
        return pltpu.make_async_remote_copy(
            src_ref=buf.at[l, :, pl.ds(PAD + s * chunk, chunk), :],
            dst_ref=halo_ref.at[h, side, :, pl.ds(s * chunk, chunk), :],
            send_sem=send_sem.at[h, side, s],
            recv_sem=recv_sem.at[h, side, s],
            device_id={"tile": to},
            device_id_type=MESH,
        )

    def halo_start(h, buf, side, s):
        @pl.when(has_right if side == 0 else has_left)
        def _():
            halo_copy(h, buf, side, s).start()

    def halo_wait(h, buf, side, s):
        @pl.when(has_left if side == 0 else has_right)
        def _():
            halo_copy(h, buf, side, s).wait_recv()

    def halo_sent(h, buf, side):
        @pl.when(has_right if side == 0 else has_left)
        def _():
            for s in range(srcs):
                halo_copy(h, buf, side, s).wait_send()

    for copy, l in zip(edge_loads, (0, last)):
        copy.wait()
        pack_guess(l)

    peers = has_left.astype(jnp.int32) + has_right.astype(jnp.int32) + (srcs - 1)
    pl.semaphore_wait(barrier, peers)

    for s in range(srcs):
        for side in range(2):
            halo_start(0, b0_ref, side, s)

    cond_load.wait()
    freq = freq_ref[0]
    kappa = jnp.float32(0.0)
    for i in range(kappa_ref.shape[0]):
        kappa = kappa + jnp.where(freq == i, kappa_ref[i], jnp.float32(0.0))
    for l in range(layers):
        pi = red_odd(l)
        ce = cond_ref[l, even, :]
        co = cond_ref[l, odd, :]
        for k, cell in enumerate((jnp.where(pi, co, ce), jnp.where(pi, ce, co))):
            coupling = kappa * cell
            inverse = 1.0 / (36.0 + coupling * coupling)
            c6_ref[k, l] = 6.0 * inverse
            cc_ref[k, l] = coupling * inverse
    inner_load.wait()
    for l in range(1, last):
        pack_guess(l)

    ry = ry_ref[...]
    row = lax.broadcasted_iota(jnp.int32, (half, recv_count), 0) * 2
    for parity in range(2):
        for b in range(4):
            rows_ref[parity * half : (parity + 1) * half, b * recv_count : (b + 1) * recv_count] = (
                jnp.where(row + parity == ry + b, 1.0, 0.0).astype(BF16)
            )
    w_t = weights_ref[...]
    rx = rx_ref[...]
    rz = rz_ref[...]
    ZC = 16
    for l in range(layers):
        pi = red_odd(l)
        at = (first_x + l) - rx
        plane = jnp.zeros((16, recv_count), F32)
        for a in range(4):
            plane = jnp.where(at == a, w_t[16 * a : 16 * a + 16, :], plane)
        for c in range(2):
            vals = plane * data_ref[c : c + 1, :]
            for z0 in range(0, size_z, ZC):
                off = lax.broadcasted_iota(jnp.int32, (ZC, recv_count), 0) + z0 - rz
                for b in range(4):
                    t = jnp.zeros((ZC, recv_count), F32)
                    for k in range(4):
                        t = jnp.where(off == k, vals[4 * b + k : 4 * b + k + 1, :], t)
                    hi = t.astype(BF16)
                    lo = (t - hi.astype(F32)).astype(BF16)
                    cols = slice(b * recv_count, (b + 1) * recv_count)
                    cols_ref[c, z0 : z0 + ZC, cols] = hi
                    cols_ref[c, size_z + z0 : size_z + z0 + ZC, cols] = lo
            both = lax.dot_general(
                rows_ref[...],
                cols_ref[c],
                (((1,), (1,)), ((), ())),
                preferred_element_type=F32,
            )
            total = both[:, :size_z] + both[:, size_z:]
            se, so = total[:half], total[half:]
            src_ref[0, l, c] = jnp.where(pi, so, se)
            src_ref[1, l, c] = jnp.where(pi, se, so)

    def update(colour, h, buf, out, out_pad, l, pieces):
        up_side = red_odd(l) if colour == 0 else jnp.logical_not(red_odd(l))
        for r in (chunk * s for s in pieces):
            sums = []
            for c in range(2):
                mid = buf[l, c, PAD + r : PAD + r + chunk, :]
                s = src_ref[colour, l, c, r : r + chunk, :] + mid
                s = s + jnp.where(
                    up_side,
                    buf[l, c, PAD + r + 1 : PAD + r + 1 + chunk, :],
                    buf[l, c, PAD + r - 1 : PAD + r - 1 + chunk, :],
                )
                if l == 0:
                    s = s + halo_ref[h, 0, c, r : r + chunk, :]
                else:
                    s = s + buf[l - 1, c, PAD + r : PAD + r + chunk, :]
                if l == last:
                    s = s + halo_ref[h, 1, c, r : r + chunk, :]
                else:
                    s = s + buf[l + 1, c, PAD + r : PAD + r + chunk, :]
                s = s + jnp.where(lane == 0, 0.0, pltpu.roll(mid, 1, 1))
                s = s + jnp.where(lane == size_z - 1, 0.0, pltpu.roll(mid, size_z - 1, 1))
                sums.append(s)
            c6 = c6_ref[colour, l, r : r + chunk, :]
            cc = cc_ref[colour, l, r : r + chunk, :]
            out[l, 0, out_pad + r : out_pad + r + chunk, :] = c6 * sums[0] + cc * sums[1]
            out[l, 1, out_pad + r : out_pad + r + chunk, :] = c6 * sums[1] - cc * sums[0]

    every = range(srcs)

    def sweep(colour, h, buf, out, between=lambda: None):
        for l in range(1, last):
            update(colour, h, buf, out, PAD, l, every)
        between()
        for s in every:
            for side, l in ((0, 0), (1, last)):
                halo_wait(h, buf, side, s)
                update(colour, h, buf, out, PAD, l, (s,))
                halo_start(h + 1, out, 1 - side, s)

    sweep(0, 0, b0_ref, r1_ref)
    sweep(1, 1, r1_ref, b2_ref)

    def terms(colour, buf, out, l, slot, pieces):
        pi = red_odd(l) if colour == 0 else jnp.logical_not(red_odd(l))
        for s in pieces:
            e = pl.ds(2 * s * chunk, chunk, stride=2)
            o = pl.ds(2 * s * chunk + 1, chunk, stride=2)
            fre = jnp.where(pi, fwd_ref[0, l, o, :], fwd_ref[0, l, e, :])
            fim = jnp.where(pi, fwd_ref[1, l, o, :], fwd_ref[1, l, e, :])
            cell = jnp.where(pi, cond_ref[l, o, :], cond_ref[l, e, :])
            rows = pl.ds(PAD + s * chunk, chunk)
            value = fre * buf[l, 1, rows, :] + fim * buf[l, 0, rows, :]
            out[s, slot] = (-kappa * cell) * value

    def grad_copies(group, terms_ref, got_ref):
        copies = []
        for step in range(1, srcs):
            to = lax.rem(me + step, srcs)
            copies.append(
                pltpu.make_async_remote_copy(
                    src_ref=terms_ref.at[to],
                    dst_ref=got_ref.at[step - 1],
                    send_sem=gsend_sem.at[group, step - 1],
                    recv_sem=grecv_sem.at[group, step - 1],
                    device_id={"src": to},
                    device_id_type=MESH,
                )
            )
        return copies

    red_copies = grad_copies(0, g_red, got_red)

    def red_inner():
        fwd_load.wait()
        for l in range(1, last):
            terms(0, r3_ref, g_red, l, l - 1, every)
        for copy in red_copies:
            copy.start()

    sweep(0, 2, b2_ref, r3_ref, red_inner)
    for slot, l in enumerate((0, last)):
        terms(0, r3_ref, g_rim, l, slot, every)
    rim_copies = grad_copies(3, g_rim, got_rim)
    for copy in rim_copies:
        copy.start()

    def emit(l):
        pi = red_odd(l)
        for c in range(2):
            red = r3_ref[l, c, PAD : PAD + half, :]
            black = b0_ref[l, c, PAD : PAD + half, :]
            adj_ref[0, c, l, even, :] = jnp.where(pi, black, red)
            adj_ref[0, c, l, odd, :] = jnp.where(pi, red, black)

    for side in range(2):
        halo_sent(0, b0_ref, side)
    for l in range(1, last):
        update(1, 3, r3_ref, b0_ref, PAD, l, every)
        terms(1, b0_ref, g_in, l, l - 1, every)
    in_copies = grad_copies(1, g_in, got_in)
    for copy in in_copies:
        copy.start()
    for l in range(1, last):
        emit(l)
    def out_copy(s):
        step = lax.rem(s - me + srcs - 1, srcs)
        return pltpu.make_async_remote_copy(
            src_ref=g_out.at[s],
            dst_ref=got_out.at[step],
            send_sem=gsend_sem.at[2, step],
            recv_sem=grecv_sem.at[2, step],
            device_id={"src": s},
            device_id_type=MESH,
        )

    for s in every:
        for side, l in ((0, 0), (1, last)):
            halo_wait(3, r3_ref, side, s)
            update(1, 3, r3_ref, b0_ref, PAD, l, (s,))
            terms(1, b0_ref, g_out, l, side, (s,))

        @pl.when(me != s)
        def _():
            out_copy(s).start()

    out_copies = grad_copies(2, g_out, got_out)
    for l in (0, last):
        emit(l)

    for h, buf in ((1, r1_ref), (2, b2_ref), (3, r3_ref)):
        for side in range(2):
            halo_sent(h, buf, side)

    def summed(terms_ref, got_ref, slot):
        value = terms_ref[me, slot]
        for step in range(srcs - 1):
            value = value + got_ref[step, slot]
        return value

    def finish(l, red_ref, got_red, black_ref, got_black, slot):
        pi = red_odd(l)
        red = summed(red_ref, got_red, slot)
        black = summed(black_ref, got_black, slot)
        grad_ref[l, pl.ds(0, chunk, stride=2), :] = jnp.where(pi, black, red)
        grad_ref[l, pl.ds(1, chunk, stride=2), :] = jnp.where(pi, red, black)

    for copy in red_copies:
        copy.wait()
    for copy in in_copies:
        copy.wait()
    for l in range(1, last):
        finish(l, g_red, got_red, g_in, got_in, l - 1)
    for copy in rim_copies:
        copy.wait()
    for copy in out_copies:
        copy.wait()
    for slot, l in enumerate((0, last)):
        finish(l, g_rim, got_rim, g_out, got_out, slot)


def store_kernel(adj_ref, grad_ref, adj_hbm, grad_hbm, sem):
    parts, layers = adj_ref.shape[1:3]
    copies = [pltpu.make_async_copy(grad_ref, grad_hbm, sem.at[0])]
    for c in range(parts):
        for l in range(layers):
            copies.append(
                pltpu.make_async_copy(adj_ref.at[0, c, l], adj_hbm.at[0, c, l], sem.at[len(copies)])
            )
    for copy in copies:
        copy.start()
    for copy in copies:
        copy.wait()


def body(
    forward_field,
    adjoint_guess,
    conductivity,
    freq_kappa,
    pair_freq,
    recv_data,
    recv_weights,
    recv_x,
    recv_y,
    recv_z,
):
    pair_count, parts, layers, size_y, size_z = adjoint_guess.shape
    assert pair_count == 1
    tiles = lax.axis_size("tile")
    srcs = lax.axis_size("src")
    half = size_y // 2
    chunk = half // srcs
    recv_count = recv_x.shape[0]
    field = (layers, parts, half + 2 * PAD, size_z)
    coef = (2, layers, half, size_z)
    vmem = pl.BlockSpec(memory_space=pltpu.VMEM)
    smem = pl.BlockSpec(memory_space=pltpu.SMEM)
    hbm = pl.BlockSpec(memory_space=pltpu.HBM)

    def grads(count, depth):
        return pltpu.VMEM((count, depth, chunk, size_z), F32)

    results = pl.pallas_call(
        functools.partial(kernel, tiles, srcs),
        out_shape=(
            jax.ShapeDtypeStruct(adjoint_guess.shape, F32),
            jax.ShapeDtypeStruct((layers, size_y // srcs, size_z), F32),
        ),
        in_specs=[smem, smem, hbm, hbm, hbm, vmem, vmem, vmem, vmem, vmem],
        out_specs=(vmem, vmem),
        scratch_shapes=[
            pltpu.VMEM((parts, layers, size_y, size_z), F32),
            pltpu.VMEM((parts, layers, size_y, size_z), F32),
            pltpu.VMEM((layers, size_y, size_z), F32),
            pltpu.VMEM(field, F32),
            pltpu.VMEM(field, F32),
            pltpu.VMEM(field, F32),
            pltpu.VMEM(field, F32),
            pltpu.VMEM((4, 2, parts, half, size_z), F32),
            pltpu.VMEM((2, layers, parts, half, size_z), F32),
            pltpu.VMEM(coef, F32),
            pltpu.VMEM(coef, F32),
            pltpu.VMEM((size_y, 4 * recv_count), BF16),
            pltpu.VMEM((2, 2 * size_z, 4 * recv_count), BF16),
            grads(srcs, layers - 2),
            grads(srcs, 2),
            grads(srcs, layers - 2),
            grads(srcs, 2),
            grads(srcs - 1, layers - 2),
            grads(srcs - 1, 2),
            grads(srcs - 1, layers - 2),
            grads(srcs - 1, 2),
            pltpu.SemaphoreType.DMA((5,)),
            pltpu.SemaphoreType.DMA((4, 2, srcs)),
            pltpu.SemaphoreType.DMA((4, 2, srcs)),
            pltpu.SemaphoreType.DMA((4, srcs - 1)),
            pltpu.SemaphoreType.DMA((4, srcs - 1)),
        ],
        compiler_params=pltpu.CompilerParams(
            collective_id=0, has_side_effects=True, vmem_limit_bytes=40 << 20
        ),
    )(
        pair_freq,
        freq_kappa,
        *(
            pltpu.with_memory_space_constraint(a, pltpu.HBM)
            for a in (forward_field, adjoint_guess, conductivity, recv_data[0], recv_weights.T)
        ),
        *(pltpu.with_memory_space_constraint(a[None], pltpu.HBM) for a in (recv_x, recv_y, recv_z)),
    )
    return pl.pallas_call(
        store_kernel,
        out_shape=tuple(jax.ShapeDtypeStruct(r.shape, F32) for r in results),
        in_specs=[vmem, vmem],
        out_specs=(hbm, hbm),
        scratch_shapes=[pltpu.SemaphoreType.DMA((1 + parts * layers,))],
        compiler_params=pltpu.CompilerParams(vmem_limit_bytes=2 << 20),
    )(*results)


def solution(mesh):
    placed = (
        P(("job", "src"), None, "tile", None, None),
        P(("job", "src"), None, "tile", None, None),
        P(("job", "tile"), None, None),
        P("job"),
        P(("job", "src")),
        P(("job", "src"), None, None),
        P("job", None),
        P("job"),
        P("job"),
        P("job"),
    )
    return jax.shard_map(
        body,
        mesh=mesh,
        in_specs=placed,
        out_specs=(P(("job", "src"), None, "tile", None, None), P(("job", "tile"), "src", None)),
        check_vma=False,
    )
```
